32 devices in a mesh: cfg: 2 (over x), ta: 8 (over z, y), gz: 2 (over core).
Axes of the slice: x: 2, y: 2, z: 4, core: 2. Of those that a mesh axis runs over, the one named last changes fastest.
Arguments:
- links: float32 [16, 2, 72, 2304], P(('cfg', 'ta'), 'gz'), parts along dimension 0, may hold values from -1 to 1, as said below
Outputs:
- flowed: float32 [16, 2, 72, 2304], P(('cfg', 'ta'), 'gz'), parts along dimension 0
The draws below stay inside these ranges and needn't reach their ends.
There are 2 independent parts, one for each index of `cfg`. The reference program is written for one: setup_inputs(seed, part) draws one part's arguments, and reference() takes and returns one part's arrays. A program takes and returns all parts, laid end to end along the dimension named above; each array names one. Nothing has to cross between parts.
Inputs may be any that keep to these rules, and one draw needn't show every extreme that they name: `links`: every link is a special unitary matrix (orthonormal rows, determinant one) up to rounding.
All inputs are finite; a program needn't handle non-finite values.
Results may differ from the reference program's by a relative error of at most 0.0001.
Values sent between devices are 32-bit elements; how exact they have to be, the bound alone decides.
A program may use at most 64 MiB of HBM per device.

```python
import jax
import jax.numpy as jnp

X = 48
Y = 48
T_SIZE = 8
Z = 2


def complex_product(first, second):
    real_part = first[..., 0, :] * second[..., 0, :] - first[..., 1, :] * second[..., 1, :]
    imag_part = first[..., 0, :] * second[..., 1, :] + first[..., 1, :] * second[..., 0, :]
    return jnp.stack([real_part, imag_part], axis=-2)


def normalize_row(row_values):
    length = jnp.sqrt(jnp.sum(row_values * row_values, axis=(-3, -2), keepdims=True) + 1e-12)
    return row_values / length


def draw_links(key, part):
    key = jax.random.fold_in(key, 11)
    shape = (T_SIZE, Z, 4, 3, 3, 2, X * Y)
    raw_values = 0.5 * jax.random.normal(key, shape, jnp.float32)
    lift = 1.2
    diagonal_unit = jnp.eye(3, dtype=jnp.float32)[:, :, None, None] * jnp.array([1.0, 0.0], jnp.float32)[None, None, :, None]
    raw_values = raw_values + lift * diagonal_unit
    unit_first = normalize_row(raw_values[:, :, :, 0])
    row_second = raw_values[:, :, :, 1]
    first_re = unit_first[..., 0, :]
    first_im = unit_first[..., 1, :]
    second_re = row_second[..., 0, :]
    second_im = row_second[..., 1, :]
    inner_re = jnp.sum(first_re * second_re + first_im * second_im, axis=-2, keepdims=True)
    inner_im = jnp.sum(first_re * second_im - first_im * second_re, axis=-2, keepdims=True)
    second_re = second_re - (inner_re * first_re - inner_im * first_im)
    second_im = second_im - (inner_re * first_im + inner_im * first_re)
    unit_second = normalize_row(jnp.stack([second_re, second_im], axis=-2))
    first_one = jnp.roll(unit_first, -1, axis=-3)
    first_two = jnp.roll(unit_first, -2, axis=-3)
    second_one = jnp.roll(unit_second, -1, axis=-3)
    second_two = jnp.roll(unit_second, -2, axis=-3)
    crossed = complex_product(first_one, second_two) - complex_product(first_two, second_one)
    unit_third = crossed * jnp.array([1.0, -1.0], jnp.float32)[:, None]
    stacked = jnp.stack([unit_first, unit_second, unit_third], axis=3)
    return stacked.reshape(T_SIZE, Z, 72, X * Y)


def setup_inputs(seed: int = 0, part: int = 0) -> dict:
    key_of = jax.random.split(jax.random.key(seed), 2)
    own_keys = jax.random.split(jax.random.fold_in(key_of[1], part), 2)
    links = draw_links(jax.random.fold_in(jax.random.fold_in(key_of[1], part), 71), part)
    return dict(links=links)


flow_step = 0.05


def multiply(left_factor, right_factor):
    left_re = left_factor[..., 0, :][..., :, :, None, :]
    left_im = left_factor[..., 1, :][..., :, :, None, :]
    right_re = right_factor[..., 0, :][..., None, :, :, :]
    right_im = right_factor[..., 1, :][..., None, :, :, :]
    real_part = jnp.sum(left_re * right_re - left_im * right_im, axis=-3)
    imag_part = jnp.sum(left_re * right_im + left_im * right_re, axis=-3)
    return jnp.stack([real_part, imag_part], axis=-2)


def dagger(matrix):
    real_part = jnp.swapaxes(matrix[..., 0, :], -3, -2)
    imag_part = -jnp.swapaxes(matrix[..., 1, :], -3, -2)
    return jnp.stack([real_part, imag_part], axis=-2)


def identity_matrix():
    diagonal_unit = jnp.eye(3, dtype=jnp.float32)
    return jnp.stack([diagonal_unit, jnp.zeros_like(diagonal_unit)], axis=-1)[:, :, :, None]


def project(loop_sum):
    antiherm = 0.5 * (loop_sum - dagger(loop_sum))
    trace_sum = antiherm[..., 0, 0, :, :] + antiherm[..., 1, 1, :, :] + antiherm[..., 2, 2, :, :]
    diagonal_unit = jnp.eye(3, dtype=jnp.float32)[:, :, None, None]
    return antiherm - diagonal_unit * trace_sum[..., None, None, :, :] / 3.0


def expmap(generator):
    unit_matrix = identity_matrix()
    result = unit_matrix + generator / 8.0
    for degree in range(7, 0, -1):
        result = unit_matrix + multiply(generator, result) / float(degree)
    return result


def shifted(values, step_y, step_x):
    if step_y != 0:
        values = jnp.roll(values, -step_y * X, axis=-1)
    if step_x != 0:
        column = jnp.arange(values.shape[-1]) % X
        if step_x == 1:
            values = jnp.where(column == X - 1, jnp.roll(values, X - 1, axis=-1), jnp.roll(values, -1, axis=-1))
        else:
            values = jnp.where(column == 0, jnp.roll(values, 1 - X, axis=-1), jnp.roll(values, 1, axis=-1))
    return values


def unit_step(direction):
    return tuple(1 if position == direction else 0 for position in range(4))


def combine(first, second, factor):
    return tuple(first[position] + factor * second[position] for position in range(4))


def fetch_link(padded, direction, offset):
    inner_t = padded.shape[0] - 2
    inner_z = padded.shape[1] - 2
    window = padded[1 + offset[0]:1 + offset[0] + inner_t, 1 + offset[1]:1 + offset[1] + inner_z, direction]
    return shifted(window, offset[2], offset[3])


def forces(padded):
    anchor = (0, 0, 0, 0)
    drifts = []
    for forward in range(4):
        forward_step = unit_step(forward)
        total_sum = None
        for sideways in range(4):
            if sideways == forward:
                continue
            across = unit_step(sideways)
            beneath = combine(anchor, across, -1)
            behind = combine(forward_step, across, -1)
            upper_loop = multiply(multiply(fetch_link(padded, sideways, forward_step), dagger(fetch_link(padded, forward, across))), dagger(fetch_link(padded, sideways, anchor)))
            lower_loop = multiply(multiply(dagger(fetch_link(padded, sideways, behind)), dagger(fetch_link(padded, forward, beneath))), fetch_link(padded, sideways, beneath))
            staple = upper_loop + lower_loop
            total_sum = staple if total_sum is None else total_sum + staple
        loop_sum = multiply(fetch_link(padded, forward, anchor), total_sum)
        drifts.append(-flow_step * project(loop_sum))
    return jnp.stack(drifts, axis=2)


def periodic(lattice):
    return jnp.pad(lattice, ((1, 1), (1, 1), (0, 0), (0, 0), (0, 0), (0, 0), (0, 0)), mode="wrap")


def reference(links):
    full_shape = links.shape
    lattice = links.reshape(full_shape[0], full_shape[1], 4, 3, 3, 2, full_shape[3])
    drift_first = forces(periodic(lattice))
    section_one = multiply(expmap(0.25 * drift_first), lattice)
    drift_second = forces(periodic(section_one))
    result = multiply(expmap((8.0 / 9.0) * drift_second - (17.0 / 36.0) * drift_first), section_one)
    return result.reshape(full_shape)
```

```python
import jax
import jax.numpy as jnp
from jax import lax
from jax.experimental import pallas as pl
from jax.experimental.pallas import tpu as pltpu
from jax.sharding import PartitionSpec as P

X = 48
ROWS = 18
LANES = 128
PAD = 24
BASE = 8
HALO = 32
flow_step = 0.05


def dot3(lefts, rights, conj_left, conj_right, want=(True, True)):
    real = imag = None
    for (ar, ai), (br, bi) in zip(lefts, rights):
        if want[0]:
            first = ar * br
            second = ai * bi
            term = first + second if conj_left != conj_right else first - second
            real = term if real is None else real + term
        if want[1]:
            first = ar * bi
            second = ai * br
            if conj_left and conj_right:
                term = -(first + second)
            elif conj_left:
                term = first - second
            elif conj_right:
                term = second - first
            else:
                term = first + second
            imag = term if imag is None else imag + term
    return real, imag


def product(a, b, adj_a=False, adj_b=False, rows=3):
    out = []
    for i in range(rows):
        left = [a[k][i] if adj_a else a[i][k] for k in range(3)]
        out.append(
            [
                dot3(left, [b[j][k] if adj_b else b[k][j] for k in range(3)], adj_a, adj_b)
                for j in range(3)
            ]
        )
    return out


def antiherm_product(a, b, adj_b=False):
    def entry(i, j, want=(True, True)):
        return dot3(
            [a[i][k] for k in range(3)],
            [b[j][k] if adj_b else b[k][j] for k in range(3)],
            False,
            adj_b,
            want,
        )

    out = []
    for i in range(3):
        value = entry(i, i, (False, True))[1]
        out.append(value + value)
    for i, j in ((0, 1), (0, 2), (1, 2)):
        up = entry(i, j)
        low = entry(j, i)
        out.append(up[0] - low[0])
        out.append(up[1] + low[1])
    return out


def third_row(rows):
    a, b = rows
    out = []
    for j in range(3):
        k, m = (j + 1) % 3, (j + 2) % 3
        (pr, pi), (qr, qi) = a[k], b[m]
        (sr, si), (tr, ti) = a[m], b[k]
        out.append(
            ((pr * qr - pi * qi) - (sr * tr - si * ti), (sr * ti + si * tr) - (pr * qi + pi * qr))
        )
    return out


def expmap(q):
    d = q[:3]
    h = [(q[4], -q[3]), (q[6], -q[5]), (q[8], -q[7])]
    n = [r * r + i * i for r, i in h]
    s = [
        d[0] * d[0] + n[0] + n[1],
        d[1] * d[1] + n[0] + n[2],
        d[2] * d[2] + n[1] + n[2],
    ]
    (ar, ai), (br, bi), (cr, ci) = h
    e01 = d[0] + d[1]
    e02 = d[0] + d[2]
    e12 = d[1] + d[2]
    w_r = ar * cr - ai * ci
    w_i = ar * ci + ai * cr
    so = [
        (e01 * ar + (br * cr + bi * ci), e01 * ai + (bi * cr - br * ci)),
        (e02 * br + w_r, e02 * bi + w_i),
        (e12 * cr + (ar * br + ai * bi), e12 * ci + (ar * bi - ai * br)),
    ]
    p = 0.5 * (s[0] + s[1] + s[2])
    det = (
        d[0] * d[1] * d[2]
        + 2.0 * (w_r * br + w_i * bi)
        - d[0] * n[2]
        - d[1] * n[1]
        - d[2] * n[0]
    )
    dd = det * det
    pp = p * p
    top = dd + pp * p
    f0r = 1.0 - dd * (1.0 / 720.0 - p * (2.0 / 40320.0))
    f1r = det * (1.0 / 24.0 - p * (2.0 / 720.0) + pp * (3.0 / 40320.0))
    f2r = -0.5 + p * (1.0 / 24.0) - pp * (1.0 / 720.0) + top * (1.0 / 40320.0)
    f0i = det * (-1.0 / 6.0 + p * (1.0 / 120.0) - pp * (1.0 / 5040.0))
    f1i = 1.0 - p * (1.0 / 6.0) + pp * (1.0 / 120.0) - top * (1.0 / 5040.0)
    f2i = det * (1.0 / 120.0 - p * (2.0 / 5040.0))
    out = [[None] * 3 for _ in range(3)]
    for i in range(3):
        out[i][i] = (f0r + f1r * d[i] + f2r * s[i], f0i + f1i * d[i] + f2i * s[i])
    for (i, j), (hr, hi), (sr, si) in zip(((0, 1), (0, 2), (1, 2)), h, so):
        rr = f1r * hr + f2r * sr
        ii = f1i * hi + f2i * si
        ri = f1r * hi + f2r * si
        ir = f1i * hr + f2i * sr
        out[i][j] = (rr - ii, ri + ir)
        out[j][i] = (rr + ii, ir - ri)
    return out


def load(ref, mat, rows, count=3):
    return [
        [
            (ref[mat * 18 + (i * 3 + j) * 2, rows, :], ref[mat * 18 + (i * 3 + j) * 2 + 1, rows, :])
            for j in range(3)
        ]
        for i in range(count)
    ]


def store(ref, base, rows, matrix):
    for i, row in enumerate(matrix):
        for j, (re, im) in enumerate(row):
            ref[base + (i * 3 + j) * 2, rows, :] = re
            ref[base + (i * 3 + j) * 2 + 1, rows, :] = im


def wrap_rows(ref):
    ref[:, BASE - 1 : BASE, :] = ref[:, BASE + ROWS - 1 : BASE + ROWS, :]
    ref[:, BASE + ROWS : BASE + ROWS + 1, :] = ref[:, BASE : BASE + 1, :]


def shift_value(here, after, before, step, lane, column):
    if step == "+y":
        return pltpu.roll(jnp.where(lane >= X, here, after), LANES - X, 1)
    if step == "-y":
        return pltpu.roll(jnp.where(lane < LANES - X, here, before), X, 1)
    if step == "+x":
        near = pltpu.roll(jnp.where(lane >= 1, here, after), LANES - 1, 1)
        far = pltpu.roll(jnp.where(lane < LANES - X + 1, here, before), X - 1, 1)
        return jnp.where(column == X - 1, far, near)
    near = pltpu.roll(jnp.where(lane < LANES - 1, here, before), 1, 1)
    far = pltpu.roll(jnp.where(lane >= X - 1, here, after), LANES - X + 1, 1)
    return jnp.where(column == 0, far, near)


def shift_matrices(source, source_mat, target, target_mat, count, step):
    lane = lax.broadcasted_iota(jnp.int32, (ROWS, LANES), 1)
    row = lax.broadcasted_iota(jnp.int32, (ROWS, LANES), 0)
    column = lax.rem(row * LANES + lane, X)

    def body(group, carry):
        for inner in range(6):
            index = group * 6 + inner
            here = source[source_mat * 18 + index, BASE : BASE + ROWS, :]
            after = source[source_mat * 18 + index, BASE + 1 : BASE + ROWS + 1, :]
            before = source[source_mat * 18 + index, BASE - 1 : BASE + ROWS - 1, :]
            target[target_mat * 18 + index, 0:ROWS, :] = shift_value(
                here, after, before, step, lane, column
            )
        return carry

    lax.fori_loop(0, count * 3, body, 0)


def pack_kernel(u_ref, out_ref):
    for d in range(3):
        out_ref[:, d * ROWS : (d + 1) * ROWS, :] = u_ref[(d + 1) * 18 : (d + 1) * 18 + 12, 0:ROWS, :]


def transport_kernel(u_ref, b_ref, out_ref, field, moved, scr):
    field[:, BASE : BASE + ROWS, :] = u_ref[0:18, 0:ROWS, :]
    wrap_rows(field)
    shift_matrices(field, 0, moved, 0, 1, "+y")
    shift_matrices(field, 0, moved, 1, 1, "+x")

    def body(chunk, carry):
        rows = pl.ds(pl.multiple_of(chunk * 8, 8), 8)
        time_link = load(u_ref, 0, rows)
        for d in range(3):
            ahead = load(b_ref, 0, rows) if d == 0 else load(moved, d - 1, rows)
            right = product(load(u_ref, d + 1, rows), ahead)
            store(scr, d * 12, rows, product(time_link, right, adj_a=True, rows=2))
        return carry

    lax.fori_loop(0, 3, body, 0)
    for d in range(3):
        out_ref[:, d * ROWS : (d + 1) * ROWS, :] = scr[d * 12 : d * 12 + 12, 0:ROWS, :]


def unpack(ref, source_row, target, mat):
    for e in range(12):
        target[mat * 18 + e, 0:ROWS, :] = ref[e, source_row : source_row + ROWS, :]


def rebuild(target, mats, rows):
    for mat in mats:
        last = third_row(load(target, mat, rows, 2))
        store(target, mat * 18 + 12, rows, [last])


def section_kernel(
    second, u_ref, b_ref, t_ref, w_ref, c_ref, *rest
):
    if second:
        d_ref, out_ref = rest[:2]
        rest = rest[2:]
    else:
        out_ref, drift_ref, pack_ref = rest[:3]
        rest = rest[3:]
    field, sib, fx, fy, halo, low, lowm, force = rest
    field[:, BASE : BASE + ROWS, :] = u_ref[:, 0:ROWS, :]
    wrap_rows(field)
    sib[:, BASE : BASE + ROWS, :] = b_ref[18:36, 0:ROWS, :]
    wrap_rows(sib)
    for d in range(3):
        unpack(t_ref, d * ROWS, halo, d)
        unpack(w_ref, d * ROWS, halo, 3 + d)
    unpack(c_ref, 0, halo, 6)
    shift_matrices(field, 0, fx, 0, 3, "+x")
    shift_matrices(sib, 0, fx, 3, 1, "+x")
    shift_matrices(field, 0, fy, 0, 2, "+y")
    shift_matrices(field, 3, fy, 2, 1, "+y")
    shift_matrices(sib, 0, fy, 3, 1, "+y")

    def planes(chunk, carry):
        rows = pl.ds(pl.multiple_of(chunk * 8, 8), 8)
        inner = pl.ds(pl.multiple_of(chunk * 8 + BASE, 8), 8)
        rebuild(halo, range(7), rows)

        def link(mu, nu):
            if nu == 0:
                return load(halo, mu - 1, rows)
            if nu == 1:
                return load(b_ref, mu, rows)
            if nu == 2:
                return load(fy, {0: 0, 1: 1, 3: 2}[mu], rows)
            return load(fx, mu, rows)

        totals = [None] * 4
        for mu, nu in ((0, 1), (0, 2), (0, 3), (1, 2), (1, 3), (2, 3)):
            first = load(u_ref, mu, rows)
            other = load(u_ref, nu, rows)
            near = product(first, link(nu, mu))
            far = product(other, link(mu, nu))
            loop = antiherm_product(near, far, adj_b=True)
            if totals[mu] is None:
                totals[mu] = loop
            else:
                totals[mu] = [a + b for a, b in zip(totals[mu], loop)]
            if totals[nu] is None:
                totals[nu] = [-b for b in loop]
            else:
                totals[nu] = [a - b for a, b in zip(totals[nu], loop)]
            if nu == 2:
                store(low, (3 + mu) * 18, inner, product(near, other, adj_a=True))
            if nu == 3:
                store(low, mu * 18, inner, product(near, other, adj_a=True))
            if (mu, nu) == (2, 3):
                store(low, 5 * 18, inner, product(far, first, adj_a=True))
        for mu in range(4):
            for k in range(9):
                force[mu * 9 + k, rows, :] = totals[mu][k]
        return carry

    lax.fori_loop(0, 3, planes, 0)
    wrap_rows(low)
    shift_matrices(low, 0, lowm, 0, 3, "-x")
    shift_matrices(low, 3, lowm, 3, 3, "-y")

    def finish(chunk, carry):
        rows = pl.ds(pl.multiple_of(chunk * 8, 8), 8)
        for mu in range(4):
            parts = []
            if mu != 1:
                ahead = (
                    load(halo, 6, rows)
                    if mu == 0
                    else load(fy, 3, rows)
                    if mu == 2
                    else load(fx, 3, rows)
                )
                inner = product(load(b_ref, mu, rows), load(b_ref, 1, rows), adj_a=True)
                parts.append(product(ahead, inner, adj_a=True))
            if mu != 3:
                parts.append(load(lowm, mu, rows))
            if mu != 2:
                parts.append(load(lowm, {0: 3, 1: 4, 3: 5}[mu], rows))
            total = parts[0]
            for part in parts[1:]:
                total = [
                    [(a[0] + b[0], a[1] + b[1]) for a, b in zip(ra, rb)]
                    for ra, rb in zip(total, part)
                ]
            if mu != 0:
                moved = load(halo, 2 + mu, rows)
                total = [
                    [
                        (total[i][j][0] + moved[j][i][0], total[i][j][1] - moved[j][i][1])
                        for j in range(3)
                    ]
                    for i in range(3)
                ]
            own = load(u_ref, mu, rows)
            loop = antiherm_product(own, total)
            loop = [loop[k] + force[mu * 9 + k, rows, :] for k in range(9)]
            mean = (loop[0] + loop[1] + loop[2]) * (1.0 / 3.0)
            loop = [loop[k] - mean if k < 3 else loop[k] for k in range(9)]
            if second:
                generator = [
                    loop[k] * (-0.5 * flow_step * 8.0 / 9.0)
                    - (17.0 / 36.0) * d_ref[mu * 9 + k, rows, :]
                    for k in range(9)
                ]
            else:
                drift = [value * (-0.5 * flow_step) for value in loop]
                for k in range(9):
                    drift_ref[mu * 9 + k, rows, :] = drift[k]
                generator = [0.25 * value for value in drift]
            store(out_ref, mu * 18, rows, product(expmap(generator), own))
        return carry

    lax.fori_loop(0, 3, finish, 0)
    if not second:
        pack_kernel(out_ref, pack_ref)


VM = pl.BlockSpec(memory_space=pltpu.VMEM)


def f32(*shape):
    return jax.ShapeDtypeStruct(shape, jnp.float32)


def call(kernel, outs, inputs, scratch):
    return pl.pallas_call(
        kernel,
        out_shape=outs,
        in_specs=[VM] * len(inputs),
        out_specs=jax.tree.map(lambda _: VM, outs),
        scratch_shapes=[pltpu.VMEM(shape, jnp.float32) for shape in scratch],
        compiler_params=pltpu.CompilerParams(vmem_limit_bytes=40 * 2**20),
    )(*inputs)


def section(links, pack, drift):
    count = lax.axis_size("ta")
    forward = [(i, (i + 1) % count) for i in range(count)]
    backward = [(target, source) for source, target in forward]
    swap = [(0, 1), (1, 0)]
    sibling = lax.ppermute(links, "gz", swap)
    ahead = lax.ppermute(pack, "ta", backward)
    transported = call(
        transport_kernel,
        f32(12, 3 * ROWS, LANES),
        [links, sibling],
        [(18, HALO, LANES), (36, PAD, LANES), (36, PAD, LANES)],
    )
    behind = lax.ppermute(transported, "ta", forward)
    corner = lax.ppermute(ahead[:, :ROWS], "gz", swap)
    inputs = [links, sibling, ahead, behind, corner]
    scratch = [
        (72, HALO, LANES),
        (18, HALO, LANES),
        (72, PAD, LANES),
        (72, PAD, LANES),
        (126, PAD, LANES),
        (108, HALO, LANES),
        (108, PAD, LANES),
        (36, PAD, LANES),
    ]
    if drift is None:
        outs = [f32(72, PAD, LANES), f32(36, PAD, LANES), f32(12, 3 * ROWS, LANES)]
        kernel = lambda *refs: section_kernel(False, *refs)
    else:
        outs = f32(72, PAD, LANES)
        inputs.append(drift)
        kernel = lambda *refs: section_kernel(True, *refs)
    return call(kernel, outs, inputs, scratch)


def shards(links):
    full_shape = links.shape
    first = jnp.pad(links.reshape(72, ROWS, LANES), ((0, 0), (0, PAD - ROWS), (0, 0)))
    pack = call(pack_kernel, f32(12, 3 * ROWS, LANES), [first], [])
    middle, drift, pack = section(first, pack, None)
    result = section(middle, pack, drift)
    return result[:, :ROWS].reshape(full_shape)


def solution(mesh):
    in_specs = (P(("cfg", "ta"), "gz", None, None),)
    out_specs = P(("cfg", "ta"), "gz", None, None)
    return jax.shard_map(shards, mesh=mesh, in_specs=in_specs, out_specs=out_specs, check_vma=False)
```

```python
import jax
import jax.numpy as jnp
from jax import lax
from jax.experimental import pallas as pl
from jax.experimental.pallas import tpu as pltpu
from jax.sharding import PartitionSpec as P

X = 48
ROWS = 18
LANES = 128
PAD = 24
BASE = 8
HALO = 32
flow_step = 0.05


def dot3(lefts, rights, conj_left, conj_right, want=(True, True)):
    real = imag = None
    for (ar, ai), (br, bi) in zip(lefts, rights):
        if want[0]:
            first = ar * br
            second = ai * bi
            term = first + second if conj_left != conj_right else first - second
            real = term if real is None else real + term
        if want[1]:
            first = ar * bi
            second = ai * br
            if conj_left and conj_right:
                term = -(first + second)
            elif conj_left:
                term = first - second
            elif conj_right:
                term = second - first
            else:
                term = first + second
            imag = term if imag is None else imag + term
    return real, imag


def product(a, b, adj_a=False, adj_b=False, rows=3):
    out = []
    for i in range(rows):
        left = [a[k][i] if adj_a else a[i][k] for k in range(3)]
        out.append(
            [
                dot3(left, [b[j][k] if adj_b else b[k][j] for k in range(3)], adj_a, adj_b)
                for j in range(3)
            ]
        )
    return out


def antiherm_product(a, b, adj_b=False):
    def entry(i, j, want=(True, True)):
        return dot3(
            [a[i][k] for k in range(3)],
            [b[j][k] if adj_b else b[k][j] for k in range(3)],
            False,
            adj_b,
            want,
        )

    out = []
    for i in range(3):
        value = entry(i, i, (False, True))[1]
        out.append(value + value)
    for i, j in ((0, 1), (0, 2), (1, 2)):
        up = entry(i, j)
        low = entry(j, i)
        out.append(up[0] - low[0])
        out.append(up[1] + low[1])
    return out


def third_row(rows):
    a, b = rows
    out = []
    for j in range(3):
        k, m = (j + 1) % 3, (j + 2) % 3
        (pr, pi), (qr, qi) = a[k], b[m]
        (sr, si), (tr, ti) = a[m], b[k]
        out.append(
            ((pr * qr - pi * qi) - (sr * tr - si * ti), (sr * ti + si * tr) - (pr * qi + pi * qr))
        )
    return out


def expmap(q):
    d = q[:3]
    h = [(q[4], -q[3]), (q[6], -q[5]), (q[8], -q[7])]
    n = [r * r + i * i for r, i in h]
    s = [
        d[0] * d[0] + n[0] + n[1],
        d[1] * d[1] + n[0] + n[2],
        d[2] * d[2] + n[1] + n[2],
    ]
    (ar, ai), (br, bi), (cr, ci) = h
    e01 = d[0] + d[1]
    e02 = d[0] + d[2]
    e12 = d[1] + d[2]
    w_r = ar * cr - ai * ci
    w_i = ar * ci + ai * cr
    so = [
        (e01 * ar + (br * cr + bi * ci), e01 * ai + (bi * cr - br * ci)),
        (e02 * br + w_r, e02 * bi + w_i),
        (e12 * cr + (ar * br + ai * bi), e12 * ci + (ar * bi - ai * br)),
    ]
    p = 0.5 * (s[0] + s[1] + s[2])
    det = (
        d[0] * d[1] * d[2]
        + 2.0 * (w_r * br + w_i * bi)
        - d[0] * n[2]
        - d[1] * n[1]
        - d[2] * n[0]
    )
    dd = det * det
    pp = p * p
    top = dd + pp * p
    f0r = 1.0 - dd * (1.0 / 720.0 - p * (2.0 / 40320.0))
    f1r = det * (1.0 / 24.0 - p * (2.0 / 720.0) + pp * (3.0 / 40320.0))
    f2r = -0.5 + p * (1.0 / 24.0) - pp * (1.0 / 720.0) + top * (1.0 / 40320.0)
    f0i = det * (-1.0 / 6.0 + p * (1.0 / 120.0) - pp * (1.0 / 5040.0))
    f1i = 1.0 - p * (1.0 / 6.0) + pp * (1.0 / 120.0) - top * (1.0 / 5040.0)
    f2i = det * (1.0 / 120.0 - p * (2.0 / 5040.0))
    out = [[None] * 3 for _ in range(3)]
    for i in range(3):
        out[i][i] = (f0r + f1r * d[i] + f2r * s[i], f0i + f1i * d[i] + f2i * s[i])
    for (i, j), (hr, hi), (sr, si) in zip(((0, 1), (0, 2), (1, 2)), h, so):
        rr = f1r * hr + f2r * sr
        ii = f1i * hi + f2i * si
        ri = f1r * hi + f2r * si
        ir = f1i * hr + f2i * sr
        out[i][j] = (rr - ii, ri + ir)
        out[j][i] = (rr + ii, ir - ri)
    return out


def load(ref, mat, rows, count=3):
    return [
        [
            (ref[mat * 18 + (i * 3 + j) * 2, rows, :], ref[mat * 18 + (i * 3 + j) * 2 + 1, rows, :])
            for j in range(3)
        ]
        for i in range(count)
    ]


def store(ref, base, rows, matrix):
    for i, row in enumerate(matrix):
        for j, (re, im) in enumerate(row):
            ref[base + (i * 3 + j) * 2, rows, :] = re
            ref[base + (i * 3 + j) * 2 + 1, rows, :] = im


def wrap_rows(ref, mat, count):
    span = slice(mat * 18, (mat + count) * 18)
    ref[span, BASE - 1 : BASE, :] = ref[span, BASE + ROWS - 1 : BASE + ROWS, :]
    ref[span, BASE + ROWS : BASE + ROWS + 1, :] = ref[span, BASE : BASE + 1, :]


def shift_value(here, after, before, step, lane, column):
    if step == "+y":
        return pltpu.roll(jnp.where(lane >= X, here, after), LANES - X, 1)
    if step == "-y":
        return pltpu.roll(jnp.where(lane < LANES - X, here, before), X, 1)
    if step == "+x":
        near = pltpu.roll(jnp.where(lane >= 1, here, after), LANES - 1, 1)
        far = pltpu.roll(jnp.where(lane < LANES - X + 1, here, before), X - 1, 1)
        return jnp.where(column == X - 1, far, near)
    near = pltpu.roll(jnp.where(lane < LANES - 1, here, before), 1, 1)
    far = pltpu.roll(jnp.where(lane >= X - 1, here, after), LANES - X + 1, 1)
    return jnp.where(column == 0, far, near)


def shift_matrices(source, source_mat, target, target_mat, count, step):
    lane = lax.broadcasted_iota(jnp.int32, (ROWS, LANES), 1)
    row = lax.broadcasted_iota(jnp.int32, (ROWS, LANES), 0)
    column = lax.rem(row * LANES + lane, X)

    def body(group, carry):
        for inner in range(6):
            index = group * 6 + inner
            here = source[source_mat * 18 + index, BASE : BASE + ROWS, :]
            after = source[source_mat * 18 + index, BASE + 1 : BASE + ROWS + 1, :]
            before = source[source_mat * 18 + index, BASE - 1 : BASE + ROWS - 1, :]
            target[target_mat * 18 + index, 0:ROWS, :] = shift_value(
                here, after, before, step, lane, column
            )
        return carry

    lax.fori_loop(0, count * 3, body, 0)


KEPT = (0, 1, 3, 4, 5, 6, 7, 8)


def load_nine(ref, base, rows):
    kept = [ref[base + k, rows, :] for k in range(8)]
    return kept[:2] + [-(kept[0] + kept[1])] + kept[2:]


def traceless(loop):
    mean = (loop[0] + loop[1] + loop[2]) * (1.0 / 3.0)
    return [loop[k] - mean if k < 3 else loop[k] for k in range(9)]


def add_matrices(first, other):
    return [
        [(a[0] + b[0], a[1] + b[1]) for a, b in zip(ra, rb)] for ra, rb in zip(first, other)
    ]


def chunks(body):
    def step(chunk, carry):
        rows = pl.ds(pl.multiple_of(chunk * 8, 8), 8)
        inner = pl.ds(pl.multiple_of(chunk * 8 + BASE, 8), 8)
        body(rows, inner)
        return carry

    lax.fori_loop(0, 3, step, 0)


def pack_rows(target, slot, source, entries):
    for position, entry in enumerate(entries):
        target[slot, position * ROWS : (position + 1) * ROWS, :] = source[entry, 0:ROWS, :]


def unpack_rows(source, slot, target, base, count):
    for e in range(count):
        target[base + e, 0:ROWS, :] = source[slot, e * ROWS : (e + 1) * ROWS, :]


def section_kernel(second, *refs):
    if second:
        u_ref, d_ref, halo_in, out_ref = refs[:4]
        refs = refs[4:]
    else:
        u_ref, out_ref, drift_ref, halo_out = refs[:4]
        refs = refs[4:]
    (field, sib, zfield, fx, fy, halo, corner, carried, low, lowm, staple, force,
     face_send, face_recv, loop_send, loop_recv, loops, arrived, send_sem, recv_sem) = refs
    if not second:
        halo = halo_out
    count = lax.axis_size("ta")
    time = lax.axis_index("ta")
    after = {"ta": lax.rem(time + 1, count)}
    before = {"ta": lax.rem(time + count - 1, count)}
    partner = {"gz": 1 - lax.axis_index("gz")}

    barrier = pltpu.get_barrier_semaphore()
    for device in (after, before, partner):
        pl.semaphore_signal(barrier, inc=1, device_id=device, device_id_type=pl.DeviceIdType.MESH)

    def remote(source, target, index, device):
        return pltpu.make_async_remote_copy(
            src_ref=source,
            dst_ref=target,
            send_sem=send_sem.at[index],
            recv_sem=recv_sem.at[index],
            device_id=device,
            device_id_type=pl.DeviceIdType.MESH,
        )

    for d in range(3):
        if second:
            pack_rows(face_send, d, d_ref, [(d + 1) * 9 + k for k in KEPT])
        else:
            pack_rows(face_send, d, u_ref, range((d + 1) * 18, (d + 1) * 18 + 12))
    pl.semaphore_wait(barrier, 3)
    faces = [remote(face_send.at[d], face_recv.at[d], 1 + d, before) for d in range(3)]
    whole = remote(u_ref, sib, 0, partner)
    whole.start()
    for copy in faces:
        copy.start()

    field[:, BASE : BASE + ROWS, :] = u_ref[:, 0:ROWS, :]
    wrap_rows(field, 0, 4)
    shift_matrices(field, 0, fx, 0, 3, "+x")
    shift_matrices(field, 0, fy, 0, 2, "+y")
    shift_matrices(field, 3, fy, 2, 1, "+y")

    whole.wait_recv()
    zfield[:, BASE : BASE + ROWS, :] = sib[18:36, 0:ROWS, :]
    wrap_rows(zfield, 0, 1)
    shift_matrices(zfield, 0, fx, 3, 1, "+x")
    shift_matrices(zfield, 0, fy, 3, 1, "+y")

    def transport(rows, inner):
        time_link = load(u_ref, 0, rows)
        for d in range(3):
            ahead = load((sib, fy, fx)[d], 0, rows)
            right = product(load(u_ref, d + 1, rows), ahead)
            store(carried, d * 18, rows, product(time_link, right, adj_a=True))

    chunks(transport)

    def link(mu, nu, rows):
        if nu == 0:
            return load(halo, mu - 1, rows)
        if nu == 1:
            return load(sib, mu, rows)
        if nu == 2:
            return load(fy, {0: 0, 1: 1, 3: 2}[mu], rows)
        return load(fx, mu, rows)

    def plane(mu, nu, totals, rows, inner):
        first = load(u_ref, mu, rows)
        other = load(u_ref, nu, rows)
        near = product(first, link(nu, mu, rows))
        far = product(other, link(mu, nu, rows))
        loop = antiherm_product(near, far, adj_b=True)
        for which, sign in ((mu, 1), (nu, -1)):
            old = totals[which]
            if old is None:
                totals[which] = loop if sign == 1 else [-b for b in loop]
            elif sign == 1:
                totals[which] = [a + b for a, b in zip(old, loop)]
            else:
                totals[which] = [a - b for a, b in zip(old, loop)]
        if nu == 2:
            store(low, (3 + mu) * 18, inner, product(near, other, adj_a=True))
        if nu == 3:
            store(low, mu * 18, inner, product(near, other, adj_a=True))
        if (mu, nu) == (2, 3):
            store(low, 5 * 18, inner, product(far, first, adj_a=True))

    def space_planes(rows, inner):
        totals = [None] * 4
        for mu, nu in ((1, 2), (1, 3), (2, 3)):
            plane(mu, nu, totals, rows, inner)
        for mu in range(1, 4):
            for k in range(9):
                force[mu * 9 + k, rows, :] = totals[mu][k]
        for mu in (2, 3):
            right = product(load(sib, mu, rows), load(sib, 1, rows), adj_a=True)
            ahead = load((fy, fx)[mu - 2], 3, rows)
            store(staple, mu * 18, rows, product(ahead, right, adj_a=True))
        store(staple, 0, rows, product(load(sib, 0, rows), load(sib, 1, rows), adj_a=True))

    chunks(space_planes)
    wrap_rows(low, 1, 2)
    wrap_rows(low, 4, 2)
    shift_matrices(low, 1, lowm, 1, 2, "-x")
    shift_matrices(low, 4, lowm, 4, 2, "-y")

    sends = []
    edge = remote(halo.at[pl.ds(0, 18)], corner, 7, partner)
    for d in range(3):
        faces[d].wait_recv()
        if second:
            unpack_rows(face_recv, d, arrived, d * 8, 8)
        else:
            unpack_rows(face_recv, d, halo, d * 18, 12)

        def rebuild(rows, inner):
            if second:
                drift = load_nine(arrived, d * 8, rows)
                moved = product(expmap([0.25 * v for v in drift]), load(halo_in, d, rows))
                store(halo, d * 18, rows, moved)
            else:
                moved = load(halo, d, rows, 2)
                moved.append(third_row(moved))
                store(halo, d * 18 + 12, rows, moved[2:])
            loop = traceless(antiherm_product(moved, load(carried, d, rows), adj_b=True))
            for position, k in enumerate(KEPT):
                loops[d * 8 + position, rows, :] = loop[k]

        chunks(rebuild)
        pack_rows(loop_send, d, loops, range(d * 8, d * 8 + 8))
        sends.append(remote(loop_send.at[d], loop_recv.at[d], 4 + d, after))
        sends[d].start()
        if d == 0:
            edge.start()

    def time_planes(rows, inner):
        totals = [None] + [[force[mu * 9 + k, rows, :] for k in range(9)] for mu in range(1, 4)]
        for nu in range(1, 4):
            plane(0, nu, totals, rows, inner)
        for mu in range(4):
            for k in range(9):
                force[mu * 9 + k, rows, :] = totals[mu][k]

    chunks(time_planes)
    wrap_rows(low, 0, 1)
    wrap_rows(low, 3, 1)
    shift_matrices(low, 0, lowm, 0, 1, "-x")
    shift_matrices(low, 3, lowm, 3, 1, "-y")
    edge.wait_recv()

    def lower_loops(rows, inner):
        for mu in range(4):
            parts = []
            if mu == 0:
                parts.append(product(load(corner, 0, rows), load(staple, 0, rows), adj_a=True))
            elif mu != 1:
                parts.append(load(staple, mu, rows))
            if mu != 3:
                parts.append(load(lowm, mu, rows))
            if mu != 2:
                parts.append(load(lowm, {0: 3, 1: 4, 3: 5}[mu], rows))
            total = parts[0]
            for part in parts[1:]:
                total = add_matrices(total, part)
            loop = antiherm_product(load(u_ref, mu, rows), total)
            for k in range(9):
                force[mu * 9 + k, rows, :] += loop[k]

    chunks(lower_loops)

    def finish_link(mu, rows):
        loop = [force[mu * 9 + k, rows, :] for k in range(9)]
        if mu != 0:
            extra = load_nine(arrived, (mu - 1) * 8, rows)
            loop = [a + b for a, b in zip(loop, extra)]
        loop = traceless(loop)
        if second:
            generator = [
                loop[k] * (-0.5 * flow_step * 8.0 / 9.0)
                - (17.0 / 36.0) * d_ref[mu * 9 + k, rows, :]
                for k in range(9)
            ]
        else:
            drift = [value * (-0.5 * flow_step) for value in loop]
            for k in range(9):
                drift_ref[mu * 9 + k, rows, :] = drift[k]
            generator = [0.25 * value for value in drift]
        store(out_ref, mu * 18, rows, product(expmap(generator), load(u_ref, mu, rows)))

    chunks(lambda rows, inner: finish_link(0, rows))
    for d in range(3):
        sends[d].wait_recv()
        unpack_rows(loop_recv, d, arrived, d * 8, 8)
        chunks(lambda rows, inner: finish_link(d + 1, rows))
    for copy in [whole, edge] + faces + sends:
        copy.wait_send()


VM = pl.BlockSpec(memory_space=pltpu.VMEM)


def f32(*shape):
    return jax.ShapeDtypeStruct(shape, jnp.float32)


def section(inputs, outs, second):
    face = (8 if second else 12) * ROWS
    shapes = [
        (72, HALO, LANES),
        (72, PAD, LANES),
        (18, HALO, LANES),
        (72, PAD, LANES),
        (72, PAD, LANES),
        (54 if second else 1, PAD, LANES),
        (18, PAD, LANES),
        (54, PAD, LANES),
        (108, HALO, LANES),
        (108, PAD, LANES),
        (72, PAD, LANES),
        (36, PAD, LANES),
        (3, face, LANES),
        (3, face, LANES),
        (3, 8 * ROWS, LANES),
        (3, 8 * ROWS, LANES),
        (24, PAD, LANES),
        (24, PAD, LANES),
    ]

    def kernel(*refs):
        section_kernel(second, *refs)

    return pl.pallas_call(
        kernel,
        out_shape=outs,
        in_specs=[VM] * len(inputs),
        out_specs=jax.tree.map(lambda _: VM, outs),
        scratch_shapes=[pltpu.VMEM(shape, jnp.float32) for shape in shapes]
        + [pltpu.SemaphoreType.DMA((8,)), pltpu.SemaphoreType.DMA((8,))],
        compiler_params=pltpu.CompilerParams(
            vmem_limit_bytes=40 * 2**20,
            collective_id=int(second),
            has_side_effects=True,
        ),
    )(*inputs)


def shards(links):
    full_shape = links.shape
    first = jnp.pad(links.reshape(72, ROWS, LANES), ((0, 0), (0, PAD - ROWS), (0, 0)))
    middle, drift, halo = section(
        [first], [f32(72, PAD, LANES), f32(36, PAD, LANES), f32(54, PAD, LANES)], False
    )
    result = section([middle, drift, halo], f32(72, PAD, LANES), True)
    return result[:, :ROWS].reshape(full_shape)


def solution(mesh):
    in_specs = (P(("cfg", "ta"), "gz", None, None),)
    out_specs = P(("cfg", "ta"), "gz", None, None)
    return jax.shard_map(shards, mesh=mesh, in_specs=in_specs, out_specs=out_specs, check_vma=False)
```

```python
import jax
import jax.numpy as jnp
from jax import lax
from jax.experimental import pallas as pl
from jax.experimental.pallas import tpu as pltpu
from jax.sharding import PartitionSpec as P

X = 48
ROWS = 18
LANES = 128
PAD = 24
BASE = 8
HALO = 32
flow_step = 0.05


def dot3(lefts, rights, conj_left, conj_right, want=(True, True)):
    real = imag = None
    for (ar, ai), (br, bi) in zip(lefts, rights):
        if want[0]:
            first = ar * br
            second = ai * bi
            term = first + second if conj_left != conj_right else first - second
            real = term if real is None else real + term
        if want[1]:
            first = ar * bi
            second = ai * br
            if conj_left and conj_right:
                term = -(first + second)
            elif conj_left:
                term = first - second
            elif conj_right:
                term = second - first
            else:
                term = first + second
            imag = term if imag is None else imag + term
    return real, imag


def product(a, b, adj_a=False, adj_b=False, rows=3):
    out = []
    for i in range(rows):
        left = [a[k][i] if adj_a else a[i][k] for k in range(3)]
        out.append(
            [
                dot3(left, [b[j][k] if adj_b else b[k][j] for k in range(3)], adj_a, adj_b)
                for j in range(3)
            ]
        )
    return out


def antiherm_product(a, b, adj_b=False):
    def entry(i, j, want=(True, True)):
        return dot3(
            [a[i][k] for k in range(3)],
            [b[j][k] if adj_b else b[k][j] for k in range(3)],
            False,
            adj_b,
            want,
        )

    out = []
    for i in range(3):
        value = entry(i, i, (False, True))[1]
        out.append(value + value)
    for i, j in ((0, 1), (0, 2), (1, 2)):
        up = entry(i, j)
        low = entry(j, i)
        out.append(up[0] - low[0])
        out.append(up[1] + low[1])
    return out


def third_row(rows):
    a, b = rows
    out = []
    for j in range(3):
        k, m = (j + 1) % 3, (j + 2) % 3
        (pr, pi), (qr, qi) = a[k], b[m]
        (sr, si), (tr, ti) = a[m], b[k]
        out.append(
            ((pr * qr - pi * qi) - (sr * tr - si * ti), (sr * ti + si * tr) - (pr * qi + pi * qr))
        )
    return out


def expmap(q):
    d = q[:3]
    h = [(q[4], -q[3]), (q[6], -q[5]), (q[8], -q[7])]
    n = [r * r + i * i for r, i in h]
    s = [
        d[0] * d[0] + n[0] + n[1],
        d[1] * d[1] + n[0] + n[2],
        d[2] * d[2] + n[1] + n[2],
    ]
    (ar, ai), (br, bi), (cr, ci) = h
    e01 = d[0] + d[1]
    e02 = d[0] + d[2]
    e12 = d[1] + d[2]
    w_r = ar * cr - ai * ci
    w_i = ar * ci + ai * cr
    so = [
        (e01 * ar + (br * cr + bi * ci), e01 * ai + (bi * cr - br * ci)),
        (e02 * br + w_r, e02 * bi + w_i),
        (e12 * cr + (ar * br + ai * bi), e12 * ci + (ar * bi - ai * br)),
    ]
    p = 0.5 * (s[0] + s[1] + s[2])
    det = (
        d[0] * d[1] * d[2]
        + 2.0 * (w_r * br + w_i * bi)
        - d[0] * n[2]
        - d[1] * n[1]
        - d[2] * n[0]
    )
    dd = det * det
    pp = p * p
    top = dd + pp * p
    f0r = 1.0 - dd * (1.0 / 720.0 - p * (2.0 / 40320.0))
    f1r = det * (1.0 / 24.0 - p * (2.0 / 720.0) + pp * (3.0 / 40320.0))
    f2r = -0.5 + p * (1.0 / 24.0) - pp * (1.0 / 720.0) + top * (1.0 / 40320.0)
    f0i = det * (-1.0 / 6.0 + p * (1.0 / 120.0) - pp * (1.0 / 5040.0))
    f1i = 1.0 - p * (1.0 / 6.0) + pp * (1.0 / 120.0) - top * (1.0 / 5040.0)
    f2i = det * (1.0 / 120.0 - p * (2.0 / 5040.0))
    out = [[None] * 3 for _ in range(3)]
    for i in range(3):
        out[i][i] = (f0r + f1r * d[i] + f2r * s[i], f0i + f1i * d[i] + f2i * s[i])
    for (i, j), (hr, hi), (sr, si) in zip(((0, 1), (0, 2), (1, 2)), h, so):
        rr = f1r * hr + f2r * sr
        ii = f1i * hi + f2i * si
        ri = f1r * hi + f2r * si
        ir = f1i * hr + f2i * sr
        out[i][j] = (rr - ii, ri + ir)
        out[j][i] = (rr + ii, ir - ri)
    return out


def load(ref, mat, rows, count=3):
    return [
        [
            (ref[mat * 18 + (i * 3 + j) * 2, rows, :], ref[mat * 18 + (i * 3 + j) * 2 + 1, rows, :])
            for j in range(3)
        ]
        for i in range(count)
    ]


def store(ref, base, rows, matrix):
    for i, row in enumerate(matrix):
        for j, (re, im) in enumerate(row):
            ref[base + (i * 3 + j) * 2, rows, :] = re
            ref[base + (i * 3 + j) * 2 + 1, rows, :] = im


def wrap_rows(ref, mat, count):
    span = slice(mat * 18, (mat + count) * 18)
    ref[span, BASE - 1 : BASE, :] = ref[span, BASE + ROWS - 1 : BASE + ROWS, :]
    ref[span, BASE + ROWS : BASE + ROWS + 1, :] = ref[span, BASE : BASE + 1, :]


def shift_value(here, after, before, step, lane, column):
    if step == "+y":
        return pltpu.roll(jnp.where(lane >= X, here, after), LANES - X, 1)
    if step == "-y":
        return pltpu.roll(jnp.where(lane < LANES - X, here, before), X, 1)
    if step == "+x":
        near = pltpu.roll(jnp.where(lane >= 1, here, after), LANES - 1, 1)
        far = pltpu.roll(jnp.where(lane < LANES - X + 1, here, before), X - 1, 1)
        return jnp.where(column == X - 1, far, near)
    near = pltpu.roll(jnp.where(lane < LANES - 1, here, before), 1, 1)
    far = pltpu.roll(jnp.where(lane >= X - 1, here, after), LANES - X + 1, 1)
    return jnp.where(column == 0, far, near)


def shift_matrices(source, source_mat, target, target_mat, count, step):
    lane = lax.broadcasted_iota(jnp.int32, (ROWS, LANES), 1)
    row = lax.broadcasted_iota(jnp.int32, (ROWS, LANES), 0)
    column = lax.rem(row * LANES + lane, X)

    def body(group, carry):
        for inner in range(6):
            index = group * 6 + inner
            here = source[source_mat * 18 + index, BASE : BASE + ROWS, :]
            after = source[source_mat * 18 + index, BASE + 1 : BASE + ROWS + 1, :]
            before = source[source_mat * 18 + index, BASE - 1 : BASE + ROWS - 1, :]
            target[target_mat * 18 + index, 0:ROWS, :] = shift_value(
                here, after, before, step, lane, column
            )
        return carry

    lax.fori_loop(0, count * 3, body, 0)


KEPT = (0, 1, 3, 4, 5, 6, 7, 8)


def load_nine(ref, base, rows):
    kept = [ref[base + k, rows, :] for k in range(8)]
    return kept[:2] + [-(kept[0] + kept[1])] + kept[2:]


def traceless(loop):
    mean = (loop[0] + loop[1] + loop[2]) * (1.0 / 3.0)
    return [loop[k] - mean if k < 3 else loop[k] for k in range(9)]


def add_matrices(first, other):
    return [
        [(a[0] + b[0], a[1] + b[1]) for a, b in zip(ra, rb)] for ra, rb in zip(first, other)
    ]


def chunks(body):
    def step(chunk, carry):
        rows = pl.ds(pl.multiple_of(chunk * 8, 8), 8)
        inner = pl.ds(pl.multiple_of(chunk * 8 + BASE, 8), 8)
        body(rows, inner)
        return carry

    lax.fori_loop(0, 3, step, 0)


def pack_rows(target, slot, source, entries):
    for position, entry in enumerate(entries):
        target[slot, position * ROWS : (position + 1) * ROWS, :] = source[entry, 0:ROWS, :]


def unpack_rows(source, slot, target, base, count):
    for e in range(count):
        target[base + e, 0:ROWS, :] = source[slot, e * ROWS : (e + 1) * ROWS, :]


def flow_kernel(*refs):
    links_ref, out_ref = refs[:2]
    (middle, drift_ref, field, zfield, fx, fy, carried, low, lowm, staple, force, loops, arrived,
     sib_a, sib_b, halo_a, halo_b, corner_a, corner_b, face_send_a, face_recv_a, face_send_b,
     face_recv_b, loop_send_a, loop_recv_a, loop_send_b, loop_recv_b, send_sem, recv_sem) = refs[2:]
    count = lax.axis_size("ta")
    time = lax.axis_index("ta")
    after = {"ta": lax.rem(time + 1, count)}
    before = {"ta": lax.rem(time + count - 1, count)}
    partner = {"gz": 1 - lax.axis_index("gz")}

    barrier = pltpu.get_barrier_semaphore()
    for device in (after, before, partner):
        pl.semaphore_signal(barrier, inc=1, device_id=device, device_id_type=pl.DeviceIdType.MESH)

    def remote(source, target, index, device):
        return pltpu.make_async_remote_copy(
            src_ref=source,
            dst_ref=target,
            send_sem=send_sem.at[index],
            recv_sem=recv_sem.at[index],
            device_id=device,
            device_id_type=pl.DeviceIdType.MESH,
        )

    def copies(section, u_ref, sib, halo, corner, face_send, face_recv, loop_send, loop_recv):
        base = section * 11
        whole = [
            remote(u_ref.at[pl.ds(m * 18, 18)], sib.at[pl.ds(m * 18, 18)], base + m, partner)
            for m in range(4)
        ]
        faces = [remote(face_send.at[d], face_recv.at[d], base + 4 + d, before) for d in range(3)]
        sends = [remote(loop_send.at[d], loop_recv.at[d], base + 7 + d, after) for d in range(3)]
        edge = remote(halo.at[pl.ds(0, 18)], corner, base + 10, partner)
        return whole, faces, sends, edge

    local = (field, zfield, fx, fy, carried, low, lowm, staple, force, loops, arrived, drift_ref)
    set_a = (sib_a, halo_a, corner_a, face_send_a, face_recv_a, loop_send_a, loop_recv_a)
    set_b = (sib_b, halo_b, corner_b, face_send_b, face_recv_b, loop_send_b, loop_recv_b)
    first = copies(0, links_ref, *set_a)
    second = copies(1, middle, *set_b)

    for d in range(3):
        pack_rows(face_send_a, d, links_ref, range((d + 1) * 18, (d + 1) * 18 + 12))
    pl.semaphore_wait(barrier, 3)
    for copy in first[1] + first[0]:
        copy.start()

    def announce(mu):
        second[0][mu].start()
        if mu:
            pack_rows(face_send_b, mu - 1, drift_ref, [mu * 9 + k for k in KEPT])
            second[1][mu - 1].start()

    section(False, links_ref, middle, None, local, set_a, first, announce)
    section(True, middle, out_ref, halo_a, local, set_b, second, lambda mu: None)
    for whole, faces, sends, edge in (first, second):
        for copy in whole + faces + sends + [edge]:
            copy.wait_send()


def section(second, u_ref, out_ref, halo_in, local, received, transfers, announce):
    field, zfield, fx, fy, carried, low, lowm, staple, force, loops, arrived, drift_ref = local
    sib, halo, corner, face_send, face_recv, loop_send, loop_recv = received
    whole, faces, sends, edge = transfers
    d_ref = drift_ref

    field[:, BASE : BASE + ROWS, :] = u_ref[:, 0:ROWS, :]
    wrap_rows(field, 0, 4)
    shift_matrices(field, 0, fx, 0, 3, "+x")
    shift_matrices(field, 0, fy, 0, 2, "+y")
    shift_matrices(field, 3, fy, 2, 1, "+y")

    for copy in whole[:2]:
        copy.wait_recv()
    zfield[:, BASE : BASE + ROWS, :] = sib[18:36, 0:ROWS, :]
    wrap_rows(zfield, 0, 1)
    shift_matrices(zfield, 0, fx, 3, 1, "+x")
    shift_matrices(zfield, 0, fy, 3, 1, "+y")

    def transport(rows, inner):
        time_link = load(u_ref, 0, rows)
        for d in range(3):
            ahead = load((sib, fy, fx)[d], 0, rows)
            right = product(load(u_ref, d + 1, rows), ahead)
            store(carried, d * 18, rows, product(time_link, right, adj_a=True))

    chunks(transport)
    for copy in whole[2:]:
        copy.wait_recv()

    def link(mu, nu, rows):
        if nu == 0:
            return load(halo, mu - 1, rows)
        if nu == 1:
            return load(sib, mu, rows)
        if nu == 2:
            return load(fy, {0: 0, 1: 1, 3: 2}[mu], rows)
        return load(fx, mu, rows)

    def plane(mu, nu, totals, rows, inner):
        first = load(u_ref, mu, rows)
        other = load(u_ref, nu, rows)
        near = product(first, link(nu, mu, rows))
        far = product(other, link(mu, nu, rows))
        loop = antiherm_product(near, far, adj_b=True)
        for which, sign in ((mu, 1), (nu, -1)):
            old = totals[which]
            if old is None:
                totals[which] = loop if sign == 1 else [-b for b in loop]
            elif sign == 1:
                totals[which] = [a + b for a, b in zip(old, loop)]
            else:
                totals[which] = [a - b for a, b in zip(old, loop)]
        if nu == 2:
            store(low, (3 + mu) * 18, inner, product(near, other, adj_a=True))
        if nu == 3:
            store(low, mu * 18, inner, product(near, other, adj_a=True))
        if (mu, nu) == (2, 3):
            store(low, 5 * 18, inner, product(far, first, adj_a=True))

    def space_planes(rows, inner):
        totals = [None] * 4
        for mu, nu in ((1, 2), (1, 3), (2, 3)):
            plane(mu, nu, totals, rows, inner)
        for mu in range(1, 4):
            for k in range(9):
                force[mu * 9 + k, rows, :] = totals[mu][k]
        for mu in (2, 3):
            right = product(load(sib, mu, rows), load(sib, 1, rows), adj_a=True)
            ahead = load((fy, fx)[mu - 2], 3, rows)
            store(staple, mu * 18, rows, product(ahead, right, adj_a=True))
        store(staple, 0, rows, product(load(sib, 0, rows), load(sib, 1, rows), adj_a=True))

    chunks(space_planes)
    wrap_rows(low, 1, 2)
    wrap_rows(low, 4, 2)
    shift_matrices(low, 1, lowm, 1, 2, "-x")
    shift_matrices(low, 4, lowm, 4, 2, "-y")

    for d in range(3):
        faces[d].wait_recv()
        if second:
            unpack_rows(face_recv, d, arrived, d * 8, 8)
        else:
            unpack_rows(face_recv, d, halo, d * 18, 12)

        def rebuild(rows, inner):
            if second:
                drift = load_nine(arrived, d * 8, rows)
                moved = product(expmap([0.25 * v for v in drift]), load(halo_in, d, rows))
                store(halo, d * 18, rows, moved)
            else:
                moved = load(halo, d, rows, 2)
                moved.append(third_row(moved))
                store(halo, d * 18 + 12, rows, moved[2:])
            loop = traceless(antiherm_product(moved, load(carried, d, rows), adj_b=True))
            for position, k in enumerate(KEPT):
                loops[d * 8 + position, rows, :] = loop[k]

        chunks(rebuild)
        pack_rows(loop_send, d, loops, range(d * 8, d * 8 + 8))
        sends[d].start()
        if d == 0:
            edge.start()

    def time_planes(rows, inner):
        totals = [None] + [[force[mu * 9 + k, rows, :] for k in range(9)] for mu in range(1, 4)]
        for nu in range(1, 4):
            plane(0, nu, totals, rows, inner)
        for mu in range(4):
            for k in range(9):
                force[mu * 9 + k, rows, :] = totals[mu][k]

    chunks(time_planes)
    wrap_rows(low, 0, 1)
    wrap_rows(low, 3, 1)
    shift_matrices(low, 0, lowm, 0, 1, "-x")
    shift_matrices(low, 3, lowm, 3, 1, "-y")
    edge.wait_recv()

    def lower_loops(rows, inner):
        for mu in range(4):
            parts = []
            if mu == 0:
                parts.append(product(load(corner, 0, rows), load(staple, 0, rows), adj_a=True))
            elif mu != 1:
                parts.append(load(staple, mu, rows))
            if mu != 3:
                parts.append(load(lowm, mu, rows))
            if mu != 2:
                parts.append(load(lowm, {0: 3, 1: 4, 3: 5}[mu], rows))
            total = parts[0]
            for part in parts[1:]:
                total = add_matrices(total, part)
            loop = antiherm_product(load(u_ref, mu, rows), total)
            for k in range(9):
                force[mu * 9 + k, rows, :] += loop[k]

    chunks(lower_loops)

    def finish_link(mu, rows):
        loop = [force[mu * 9 + k, rows, :] for k in range(9)]
        if mu != 0:
            extra = load_nine(arrived, (mu - 1) * 8, rows)
            loop = [a + b for a, b in zip(loop, extra)]
        loop = traceless(loop)
        if second:
            generator = [
                loop[k] * (-0.5 * flow_step * 8.0 / 9.0)
                - (17.0 / 36.0) * d_ref[mu * 9 + k, rows, :]
                for k in range(9)
            ]
        else:
            drift = [value * (-0.5 * flow_step) for value in loop]
            for k in range(9):
                drift_ref[mu * 9 + k, rows, :] = drift[k]
            generator = [0.25 * value for value in drift]
        store(out_ref, mu * 18, rows, product(expmap(generator), load(u_ref, mu, rows)))

    chunks(lambda rows, inner: finish_link(0, rows))
    announce(0)
    for d in range(3):
        sends[d].wait_recv()
        unpack_rows(loop_recv, d, arrived, d * 8, 8)
        chunks(lambda rows, inner: finish_link(d + 1, rows))
        announce(d + 1)


VM = pl.BlockSpec(memory_space=pltpu.VMEM)


def f32(*shape):
    return jax.ShapeDtypeStruct(shape, jnp.float32)


def flow(links):
    face = (3, 12 * ROWS, LANES)
    short = (3, 8 * ROWS, LANES)
    shapes = [
        (72, PAD, LANES),
        (36, PAD, LANES),
        (72, HALO, LANES),
        (18, HALO, LANES),
        (72, PAD, LANES),
        (72, PAD, LANES),
        (54, PAD, LANES),
        (108, HALO, LANES),
        (108, PAD, LANES),
        (72, PAD, LANES),
        (36, PAD, LANES),
        (24, PAD, LANES),
        (24, PAD, LANES),
        (72, PAD, LANES),
        (72, PAD, LANES),
        (54, PAD, LANES),
        (54, PAD, LANES),
        (18, PAD, LANES),
        (18, PAD, LANES),
        face,
        face,
        short,
        short,
        short,
        short,
        short,
        short,
    ]
    return pl.pallas_call(
        flow_kernel,
        out_shape=f32(72, PAD, LANES),
        in_specs=[VM],
        out_specs=VM,
        scratch_shapes=[pltpu.VMEM(shape, jnp.float32) for shape in shapes]
        + [pltpu.SemaphoreType.DMA((22,)), pltpu.SemaphoreType.DMA((22,))],
        compiler_params=pltpu.CompilerParams(
            vmem_limit_bytes=40 * 2**20, collective_id=0, has_side_effects=True
        ),
    )(links)


def shards(links):
    full_shape = links.shape
    first = jnp.pad(links.reshape(72, ROWS, LANES), ((0, 0), (0, PAD - ROWS), (0, 0)))
    return flow(first)[:, :ROWS].reshape(full_shape)


def solution(mesh):
    in_specs = (P(("cfg", "ta"), "gz", None, None),)
    out_specs = P(("cfg", "ta"), "gz", None, None)
    return jax.shard_map(shards, mesh=mesh, in_specs=in_specs, out_specs=out_specs, check_vma=False)
```

```python
import jax
import jax.numpy as jnp
from jax import lax
from jax.experimental import pallas as pl
from jax.experimental.pallas import tpu as pltpu
from jax.sharding import PartitionSpec as P

X = 48
ROWS = 18
LANES = 128
PAD = 24
BASE = 8
HALO = 32
flow_step = 0.05


def dot3(lefts, rights, conj_left, conj_right, want=(True, True)):
    real = imag = None
    for (ar, ai), (br, bi) in zip(lefts, rights):
        if want[0]:
            first = ar * br
            second = ai * bi
            term = first + second if conj_left != conj_right else first - second
            real = term if real is None else real + term
        if want[1]:
            first = ar * bi
            second = ai * br
            if conj_left and conj_right:
                term = -(first + second)
            elif conj_left:
                term = first - second
            elif conj_right:
                term = second - first
            else:
                term = first + second
            imag = term if imag is None else imag + term
    return real, imag


def product(a, b, adj_a=False, adj_b=False, rows=3):
    out = []
    for i in range(rows):
        left = [a[k][i] if adj_a else a[i][k] for k in range(3)]
        out.append(
            [
                dot3(left, [b[j][k] if adj_b else b[k][j] for k in range(3)], adj_a, adj_b)
                for j in range(3)
            ]
        )
    return out


def antiherm_product(a, b, adj_b=False):
    def entry(i, j, want=(True, True)):
        return dot3(
            [a[i][k] for k in range(3)],
            [b[j][k] if adj_b else b[k][j] for k in range(3)],
            False,
            adj_b,
            want,
        )

    out = []
    for i in range(3):
        value = entry(i, i, (False, True))[1]
        out.append(value + value)
    for i, j in ((0, 1), (0, 2), (1, 2)):
        up = entry(i, j)
        low = entry(j, i)
        out.append(up[0] - low[0])
        out.append(up[1] + low[1])
    return out


def third_row(rows):
    a, b = rows
    out = []
    for j in range(3):
        k, m = (j + 1) % 3, (j + 2) % 3
        (pr, pi), (qr, qi) = a[k], b[m]
        (sr, si), (tr, ti) = a[m], b[k]
        out.append(
            ((pr * qr - pi * qi) - (sr * tr - si * ti), (sr * ti + si * tr) - (pr * qi + pi * qr))
        )
    return out


def expmap(q):
    d = q[:3]
    h = [(q[4], -q[3]), (q[6], -q[5]), (q[8], -q[7])]
    n = [r * r + i * i for r, i in h]
    s = [
        d[0] * d[0] + n[0] + n[1],
        d[1] * d[1] + n[0] + n[2],
        d[2] * d[2] + n[1] + n[2],
    ]
    (ar, ai), (br, bi), (cr, ci) = h
    e01 = d[0] + d[1]
    e02 = d[0] + d[2]
    e12 = d[1] + d[2]
    w_r = ar * cr - ai * ci
    w_i = ar * ci + ai * cr
    so = [
        (e01 * ar + (br * cr + bi * ci), e01 * ai + (bi * cr - br * ci)),
        (e02 * br + w_r, e02 * bi + w_i),
        (e12 * cr + (ar * br + ai * bi), e12 * ci + (ar * bi - ai * br)),
    ]
    p = 0.5 * (s[0] + s[1] + s[2])
    det = (
        d[0] * d[1] * d[2]
        + 2.0 * (w_r * br + w_i * bi)
        - d[0] * n[2]
        - d[1] * n[1]
        - d[2] * n[0]
    )
    dd = det * det
    pp = p * p
    top = dd + pp * p
    f0r = 1.0 - dd * (1.0 / 720.0 - p * (2.0 / 40320.0))
    f1r = det * (1.0 / 24.0 - p * (2.0 / 720.0) + pp * (3.0 / 40320.0))
    f2r = -0.5 + p * (1.0 / 24.0) - pp * (1.0 / 720.0) + top * (1.0 / 40320.0)
    f0i = det * (-1.0 / 6.0 + p * (1.0 / 120.0) - pp * (1.0 / 5040.0))
    f1i = 1.0 - p * (1.0 / 6.0) + pp * (1.0 / 120.0) - top * (1.0 / 5040.0)
    f2i = det * (1.0 / 120.0 - p * (2.0 / 5040.0))
    out = [[None] * 3 for _ in range(3)]
    for i in range(3):
        out[i][i] = (f0r + f1r * d[i] + f2r * s[i], f0i + f1i * d[i] + f2i * s[i])
    for (i, j), (hr, hi), (sr, si) in zip(((0, 1), (0, 2), (1, 2)), h, so):
        rr = f1r * hr + f2r * sr
        ii = f1i * hi + f2i * si
        ri = f1r * hi + f2r * si
        ir = f1i * hr + f2i * sr
        out[i][j] = (rr - ii, ri + ir)
        out[j][i] = (rr + ii, ir - ri)
    return out


def load(ref, mat, rows, count=3):
    return [
        [
            (ref[mat * 18 + (i * 3 + j) * 2, rows, :], ref[mat * 18 + (i * 3 + j) * 2 + 1, rows, :])
            for j in range(3)
        ]
        for i in range(count)
    ]


def store(ref, base, rows, matrix):
    for i, row in enumerate(matrix):
        for j, (re, im) in enumerate(row):
            ref[base + (i * 3 + j) * 2, rows, :] = re
            ref[base + (i * 3 + j) * 2 + 1, rows, :] = im


def wrap_rows(ref, mat, count):
    span = slice(mat * 18, (mat + count) * 18)
    ref[span, BASE - 1 : BASE, :] = ref[span, BASE + ROWS - 1 : BASE + ROWS, :]
    ref[span, BASE + ROWS : BASE + ROWS + 1, :] = ref[span, BASE : BASE + 1, :]


def shift_value(here, after, before, step, lane, column):
    if step == "+y":
        return pltpu.roll(jnp.where(lane >= X, here, after), LANES - X, 1)
    if step == "-y":
        return pltpu.roll(jnp.where(lane < LANES - X, here, before), X, 1)
    if step == "+x":
        near = pltpu.roll(jnp.where(lane >= 1, here, after), LANES - 1, 1)
        far = pltpu.roll(jnp.where(lane < LANES - X + 1, here, before), X - 1, 1)
        return jnp.where(column == X - 1, far, near)
    near = pltpu.roll(jnp.where(lane < LANES - 1, here, before), 1, 1)
    far = pltpu.roll(jnp.where(lane >= X - 1, here, after), LANES - X + 1, 1)
    return jnp.where(column == 0, far, near)


def shift_matrices(source, source_mat, target, target_mat, count, step):
    lane = lax.broadcasted_iota(jnp.int32, (ROWS, LANES), 1)
    row = lax.broadcasted_iota(jnp.int32, (ROWS, LANES), 0)
    column = lax.rem(row * LANES + lane, X)

    def body(group, carry):
        for inner in range(6):
            index = group * 6 + inner
            here = source[source_mat * 18 + index, BASE : BASE + ROWS, :]
            after = source[source_mat * 18 + index, BASE + 1 : BASE + ROWS + 1, :]
            before = source[source_mat * 18 + index, BASE - 1 : BASE + ROWS - 1, :]
            target[target_mat * 18 + index, 0:ROWS, :] = shift_value(
                here, after, before, step, lane, column
            )
        return carry

    lax.fori_loop(0, count * 3, body, 0)


KEPT = (0, 1, 3, 4, 5, 6, 7, 8)


def load_nine(ref, base, rows):
    kept = [ref[base + k, rows, :] for k in range(8)]
    return kept[:2] + [-(kept[0] + kept[1])] + kept[2:]


def traceless(loop):
    mean = (loop[0] + loop[1] + loop[2]) * (1.0 / 3.0)
    return [loop[k] - mean if k < 3 else loop[k] for k in range(9)]


def add_matrices(first, other):
    return [
        [(a[0] + b[0], a[1] + b[1]) for a, b in zip(ra, rb)] for ra, rb in zip(first, other)
    ]


def chunks(body):
    def step(chunk, carry):
        rows = pl.ds(pl.multiple_of(chunk * 8, 8), 8)
        inner = pl.ds(pl.multiple_of(chunk * 8 + BASE, 8), 8)
        body(rows, inner)
        return carry

    lax.fori_loop(0, 3, step, 0)


def pack_rows(target, slot, source, entries):
    for position, entry in enumerate(entries):
        target[slot, position * ROWS : (position + 1) * ROWS, :] = source[entry, 0:ROWS, :]


def unpack_rows(source, slot, target, base, count):
    for e in range(count):
        target[base + e, 0:ROWS, :] = source[slot, e * ROWS : (e + 1) * ROWS, :]


def flow_kernel(*refs):
    links_ref, out_ref = refs[:2]
    (middle, drift_ref, field, zfield, fx, fy, carried, low, lowm, staple, force, loops, arrived,
     sib_a, sib_b, halo_a, halo_b, corner_a, corner_b, face_send_a, face_recv_a, face_send_b,
     face_recv_b, loop_send_a, loop_recv_a, loop_send_b, loop_recv_b, carry_send, carry_recv, send_sem, recv_sem) = refs[2:]
    count = lax.axis_size("ta")
    time = lax.axis_index("ta")
    after = {"ta": lax.rem(time + 1, count)}
    before = {"ta": lax.rem(time + count - 1, count)}
    partner = {"gz": 1 - lax.axis_index("gz")}

    barrier = pltpu.get_barrier_semaphore()
    for device in (after, before, partner):
        pl.semaphore_signal(barrier, inc=1, device_id=device, device_id_type=pl.DeviceIdType.MESH)

    def remote(source, target, index, device):
        return pltpu.make_async_remote_copy(
            src_ref=source,
            dst_ref=target,
            send_sem=send_sem.at[index],
            recv_sem=recv_sem.at[index],
            device_id=device,
            device_id_type=pl.DeviceIdType.MESH,
        )

    def copies(section, u_ref, sib, halo, corner, face_send, face_recv, loop_send, loop_recv):
        base = section * 11
        whole = [
            remote(u_ref.at[pl.ds(m * 18, 18)], sib.at[pl.ds(m * 18, 18)], base + m, partner)
            for m in range(4)
        ]
        faces = [remote(face_send.at[d], face_recv.at[d], base + 4 + d, before) for d in range(3)]
        sends = [remote(loop_send.at[d], loop_recv.at[d], base + 7 + d, after) for d in range(3)]
        edge = remote(halo.at[pl.ds(0, 18)], corner, base + 10, partner)
        return whole, faces, sends, edge

    local = (field, zfield, fx, fy, carried, low, lowm, staple, force, loops, arrived, drift_ref)
    set_a = (sib_a, halo_a, corner_a, face_send_a, face_recv_a, loop_send_a, loop_recv_a)
    set_b = (sib_b, halo_b, corner_b, face_send_b, face_recv_b, loop_send_b, loop_recv_b)
    first = copies(0, links_ref, *set_a)
    second = copies(1, middle, *set_b)
    first[2][2] = remote(carry_send, carry_recv, 9, after)

    for d in range(3):
        pack_rows(face_send_a, d, links_ref, range((d + 1) * 18, (d + 1) * 18 + 12))
    pl.semaphore_wait(barrier, 3)
    for copy in first[1] + first[0]:
        copy.start()

    def announce(mu):
        second[0][mu].start()
        if mu:
            pack_rows(face_send_b, mu - 1, drift_ref, [mu * 9 + k for k in KEPT])
            second[1][mu - 1].start()

    carry = (carry_send, carry_recv)
    section(False, links_ref, middle, None, local, set_a, first, announce, carry)
    section(True, middle, out_ref, halo_a, local, set_b, second, lambda mu: None, carry)
    for whole, faces, sends, edge in (first, second):
        for copy in whole + faces + sends + [edge]:
            copy.wait_send()


def section(second, u_ref, out_ref, halo_in, local, received, transfers, announce, carry):
    field, zfield, fx, fy, carried, low, lowm, staple, force, loops, arrived, drift_ref = local
    sib, halo, corner, face_send, face_recv, loop_send, loop_recv = received
    whole, faces, sends, edge = transfers
    d_ref = drift_ref

    field[:, BASE : BASE + ROWS, :] = u_ref[:, 0:ROWS, :]
    wrap_rows(field, 0, 4)
    shift_matrices(field, 0, fx, 0, 3, "+x")
    shift_matrices(field, 0, fy, 0, 2, "+y")
    shift_matrices(field, 3, fy, 2, 1, "+y")

    for copy in whole[:2]:
        copy.wait_recv()
    zfield[:, BASE : BASE + ROWS, :] = sib[18:36, 0:ROWS, :]
    wrap_rows(zfield, 0, 1)
    shift_matrices(zfield, 0, fx, 3, 1, "+x")
    shift_matrices(zfield, 0, fy, 3, 1, "+y")

    def transport(rows, inner):
        time_link = load(u_ref, 0, rows)
        for d in range(3):
            ahead = load((sib, fy, fx)[d], 0, rows)
            right = product(load(u_ref, d + 1, rows), ahead)
            store(carried, d * 18, rows, product(time_link, right, adj_a=True))

    chunks(transport)
    if not second:
        pack_rows(carry[0], 0, carried, range(36, 48))
        sends[2].start()
    for copy in whole[2:]:
        copy.wait_recv()

    def link(mu, nu, rows):
        if nu == 0:
            return load(halo, mu - 1, rows)
        if nu == 1:
            return load(sib, mu, rows)
        if nu == 2:
            return load(fy, {0: 0, 1: 1, 3: 2}[mu], rows)
        return load(fx, mu, rows)

    def plane(mu, nu, totals, rows, inner):
        first = load(u_ref, mu, rows)
        other = load(u_ref, nu, rows)
        near = product(first, link(nu, mu, rows))
        far = product(other, link(mu, nu, rows))
        loop = antiherm_product(near, far, adj_b=True)
        for which, sign in ((mu, 1), (nu, -1)):
            old = totals[which]
            if old is None:
                totals[which] = loop if sign == 1 else [-b for b in loop]
            elif sign == 1:
                totals[which] = [a + b for a, b in zip(old, loop)]
            else:
                totals[which] = [a - b for a, b in zip(old, loop)]
        if nu == 2:
            store(low, (3 + mu) * 18, inner, product(near, other, adj_a=True))
        if nu == 3:
            store(low, mu * 18, inner, product(near, other, adj_a=True))
        if (mu, nu) == (2, 3):
            store(low, 5 * 18, inner, product(far, first, adj_a=True))

    def space_planes(rows, inner):
        totals = [None] * 4
        for mu, nu in ((1, 2), (1, 3), (2, 3)):
            plane(mu, nu, totals, rows, inner)
        for mu in range(1, 4):
            for k in range(9):
                force[mu * 9 + k, rows, :] = totals[mu][k]
        for mu in (2, 3):
            right = product(load(sib, mu, rows), load(sib, 1, rows), adj_a=True)
            ahead = load((fy, fx)[mu - 2], 3, rows)
            store(staple, mu * 18, rows, product(ahead, right, adj_a=True))
        store(staple, 0, rows, product(load(sib, 0, rows), load(sib, 1, rows), adj_a=True))

    chunks(space_planes)
    wrap_rows(low, 1, 2)
    wrap_rows(low, 4, 2)
    shift_matrices(low, 1, lowm, 1, 2, "-x")
    shift_matrices(low, 4, lowm, 4, 2, "-y")

    for d in range(3):
        faces[d].wait_recv()
        if second:
            unpack_rows(face_recv, d, arrived, d * 8, 8)
        else:
            unpack_rows(face_recv, d, halo, d * 18, 12)

        def rebuild(rows, inner):
            if second:
                drift = load_nine(arrived, d * 8, rows)
                moved = product(expmap([0.25 * v for v in drift]), load(halo_in, d, rows))
                store(halo, d * 18, rows, moved)
            else:
                moved = load(halo, d, rows, 2)
                moved.append(third_row(moved))
                store(halo, d * 18 + 12, rows, moved[2:])
            if d == 2 and not second:
                return
            loop = traceless(antiherm_product(moved, load(carried, d, rows), adj_b=True))
            for position, k in enumerate(KEPT):
                loops[d * 8 + position, rows, :] = loop[k]

        chunks(rebuild)
        if second or d < 2:
            pack_rows(loop_send, d, loops, range(d * 8, d * 8 + 8))
            sends[d].start()
        if d == 0:
            edge.start()

    def time_planes(rows, inner):
        totals = [None] + [[force[mu * 9 + k, rows, :] for k in range(9)] for mu in range(1, 4)]
        for nu in range(1, 4):
            plane(0, nu, totals, rows, inner)
        for mu in range(4):
            for k in range(9):
                force[mu * 9 + k, rows, :] = totals[mu][k]

    chunks(time_planes)
    wrap_rows(low, 0, 1)
    wrap_rows(low, 3, 1)
    shift_matrices(low, 0, lowm, 0, 1, "-x")
    shift_matrices(low, 3, lowm, 3, 1, "-y")
    edge.wait_recv()

    def lower_loops(rows, inner):
        for mu in range(4):
            parts = []
            if mu == 0:
                parts.append(product(load(corner, 0, rows), load(staple, 0, rows), adj_a=True))
            elif mu != 1:
                parts.append(load(staple, mu, rows))
            if mu != 3:
                parts.append(load(lowm, mu, rows))
            if mu != 2:
                parts.append(load(lowm, {0: 3, 1: 4, 3: 5}[mu], rows))
            total = parts[0]
            for part in parts[1:]:
                total = add_matrices(total, part)
            loop = antiherm_product(load(u_ref, mu, rows), total)
            for k in range(9):
                force[mu * 9 + k, rows, :] += loop[k]

    chunks(lower_loops)

    def finish_link(mu, rows):
        loop = [force[mu * 9 + k, rows, :] for k in range(9)]
        if mu == 3 and not second:
            moved = load(carried, 2, rows, 2)
            moved.append(third_row(moved))
            extra = antiherm_product(load(u_ref, 3, rows), moved, adj_b=True)
            loop = [a + b for a, b in zip(loop, extra)]
        elif mu != 0:
            extra = load_nine(arrived, (mu - 1) * 8, rows)
            loop = [a + b for a, b in zip(loop, extra)]
        loop = traceless(loop)
        if second:
            generator = [
                loop[k] * (-0.5 * flow_step * 8.0 / 9.0)
                - (17.0 / 36.0) * d_ref[mu * 9 + k, rows, :]
                for k in range(9)
            ]
        else:
            drift = [value * (-0.5 * flow_step) for value in loop]
            for k in range(9):
                drift_ref[mu * 9 + k, rows, :] = drift[k]
            generator = [0.25 * value for value in drift]
        store(out_ref, mu * 18, rows, product(expmap(generator), load(u_ref, mu, rows)))

    chunks(lambda rows, inner: finish_link(0, rows))
    announce(0)
    for d in range(3):
        sends[d].wait_recv()
        if second or d < 2:
            unpack_rows(loop_recv, d, arrived, d * 8, 8)
        else:
            unpack_rows(carry[1], 0, carried, 36, 12)
        chunks(lambda rows, inner: finish_link(d + 1, rows))
        announce(d + 1)


VM = pl.BlockSpec(memory_space=pltpu.VMEM)


def f32(*shape):
    return jax.ShapeDtypeStruct(shape, jnp.float32)


def flow(links):
    face = (3, 12 * ROWS, LANES)
    short = (3, 8 * ROWS, LANES)
    shapes = [
        (72, PAD, LANES),
        (36, PAD, LANES),
        (72, HALO, LANES),
        (18, HALO, LANES),
        (72, PAD, LANES),
        (72, PAD, LANES),
        (54, PAD, LANES),
        (108, HALO, LANES),
        (108, PAD, LANES),
        (72, PAD, LANES),
        (36, PAD, LANES),
        (24, PAD, LANES),
        (24, PAD, LANES),
        (72, PAD, LANES),
        (72, PAD, LANES),
        (54, PAD, LANES),
        (54, PAD, LANES),
        (18, PAD, LANES),
        (18, PAD, LANES),
        face,
        face,
        short,
        short,
        short,
        short,
        short,
        short,
        (1, 12 * ROWS, LANES),
        (1, 12 * ROWS, LANES),
    ]
    return pl.pallas_call(
        flow_kernel,
        out_shape=f32(72, PAD, LANES),
        in_specs=[VM],
        out_specs=VM,
        scratch_shapes=[pltpu.VMEM(shape, jnp.float32) for shape in shapes]
        + [pltpu.SemaphoreType.DMA((22,)), pltpu.SemaphoreType.DMA((22,))],
        compiler_params=pltpu.CompilerParams(
            vmem_limit_bytes=40 * 2**20, collective_id=0, has_side_effects=True
        ),
    )(links)


def shards(links):
    full_shape = links.shape
    first = jnp.pad(links.reshape(72, ROWS, LANES), ((0, 0), (0, PAD - ROWS), (0, 0)))
    return flow(first)[:, :ROWS].reshape(full_shape)


def solution(mesh):
    in_specs = (P(("cfg", "ta"), "gz", None, None),)
    out_specs = P(("cfg", "ta"), "gz", None, None)
    return jax.shard_map(shards, mesh=mesh, in_specs=in_specs, out_specs=out_specs, check_vma=False)
```
